32 devices in a mesh: grp: 2 (over x), basis: 16 (over z, y, core).
Axes of the slice: x: 2, y: 2, z: 4, core: 2. Of those that a mesh axis runs over, the one named last changes fastest.
Arguments:
- query_inputs: bfloat16 [384, 4096], P(('grp', 'basis')), parts along dimension 0, may hold values from -6 to 6
- query_grads: bfloat16 [384, 14336], P(('grp', 'basis')), parts along dimension 0, may hold values from -6 to 6
- basis_in: bfloat16 [4096, 4096], P(None, 'basis'), may hold values from -0.09375 to 0.09375
- basis_out: bfloat16 [14336, 14336], P(None, 'basis'), may hold values from -0.046875 to 0.046875
- eig_in: float32 [4096], P('basis'), may hold values from 0.01 to 10
- eig_out: float32 [14336], P('basis'), may hold values from 0.01 to 10
- trace_inputs: bfloat16 [4096, 4096], P(('grp', 'basis')), parts along dimension 0, may hold values from -6 to 6
- trace_grads: bfloat16 [4096, 14336], P(('grp', 'basis')), parts along dimension 0, may hold values from -6 to 6
Outputs:
- scores: float32 [64, 64], P(None, ('grp', 'basis')), parts along dimension 1
The draws below stay inside these ranges and needn't reach their ends.
There are 2 independent parts, one for each index of `grp`. The reference program is written for one: setup_inputs(seed, part) draws one part's arguments, and reference() takes and returns one part's arrays. A program takes and returns all parts, laid end to end along the dimension named above; an argument that names none is the same for every part. Nothing has to cross between parts.
All inputs are finite; a program needn't handle non-finite values.
Results may differ from the reference program's by a relative error of at most 0.0075.
Values may be sent and summed in bfloat16 or wider, within the bound.
A program may use at most 128 MiB of HBM per device.

```python
import math
import jax
import jax.numpy as jnp
from jax import lax

DA = 4096
FW = 14336
QUERIES = 64
QTOK = 3
TTOK = 64
TRACES = 32
QROWS = 192
TROWS = 2048


def levels(rng, extent, cuts, smallest, high):
    def one(dim, shards_of):
        draws = jax.random.uniform(jax.random.fold_in(jax.random.fold_in(rng, 6), dim), (shards_of,), jnp.float32, smallest / len(cuts), high / len(cuts))
        return jnp.repeat(jnp.exp(draws), extent[dim] // shards_of).reshape((-1,) + (1,) * (len(extent) - dim - 1))

    factor_of = one(*cuts[0])
    for cut in cuts[1:]:
        factor_of = factor_of * one(*cut)
    return factor_of


def normal_values(key, dims, deviation, limit, pieces=(), dtype=jnp.bfloat16):
    array = jax.random.normal(key, dims, jnp.float32) * deviation
    if len(pieces) > 0:
        array = levels(key, dims, pieces, -0.22, 0.18) * array
    return jnp.clip(array, min=-limit, max=limit).astype(dtype)


def setup_inputs(seed: int = 0, part: int = 0) -> dict:
    keys = jax.random.split(jax.random.key(seed), 9)
    part_splits = jax.random.split(jax.random.fold_in(keys[8], part), 9)
    query_inputs = normal_values(part_splits[0], (QROWS, DA), 1.0, 6.0, ((0, 16),))
    query_grads = normal_values(part_splits[1], (QROWS, FW), 1.0, 6.0, ((0, 16),))
    basis_in = normal_values(keys[2], (DA, DA), DA ** -0.5, 0.09375, ((1, 16),))
    basis_out = normal_values(keys[3], (FW, FW), FW ** -0.5, 0.046875, ((1, 16),))
    eig_in = jnp.clip(jnp.exp(math.log(10.0) - 6.9077553 * jax.random.uniform(keys[4], (DA,), jnp.float32) ** levels(keys[4], (DA,), ((0, 16),), -0.2, 0.2)), 0.01, 10.0)
    eig_out = jnp.clip(jnp.exp(math.log(10.0) - 6.9077553 * jax.random.uniform(keys[5], (FW,), jnp.float32) ** levels(keys[5], (FW,), ((0, 16),), -0.2, 0.2)), 0.01, 10.0)
    trace_inputs = normal_values(part_splits[6], (TROWS, DA), 1.0, 6.0, ((0, 16),))
    trace_grads = normal_values(part_splits[7], (TROWS, FW), 1.0, 6.0, ((0, 16),))
    return dict(query_inputs=query_inputs, query_grads=query_grads, basis_in=basis_in, basis_out=basis_out, eig_in=eig_in, eig_out=eig_out, trace_inputs=trace_inputs, trace_grads=trace_grads)


damping = 0.1

def reference(query_inputs, query_grads, basis_in, basis_out, eig_in, eig_out, trace_inputs, trace_grads):
    rot_in = (jnp.dot(query_inputs, basis_in, preferred_element_type=jnp.float32) / (eig_in + damping)).astype(jnp.bfloat16)
    rot_grad = (jnp.dot(query_grads, basis_out, preferred_element_type=jnp.float32) / (eig_out + damping)).astype(jnp.bfloat16)
    pre_in = jnp.dot(rot_in, basis_in.T, preferred_element_type=jnp.float32)
    pre_grad = jnp.dot(rot_grad, basis_out.T, preferred_element_type=jnp.float32)
    pair_in = jnp.dot(trace_inputs.astype(jnp.float32), pre_in.T, precision=lax.Precision.HIGHEST) / math.sqrt(DA)
    pair_grad = jnp.dot(trace_grads.astype(jnp.float32), pre_grad.T, precision=lax.Precision.HIGHEST) / math.sqrt(FW)
    products = (pair_in * pair_grad).reshape(TRACES, TTOK, QUERIES, QTOK)
    return lax.optimization_barrier(jnp.sum(products, axis=(1, 3))).T / (TTOK * QTOK)
```

```python
import functools
import math

import jax
import jax.numpy as jnp
from jax import lax
from jax.experimental import pallas as pl
from jax.experimental.pallas import tpu as pltpu
from jax.sharding import PartitionSpec as P

DA = 4096
FW = 14336
QUERIES = 64
QTOK = 3
TTOK = 64
QROWS = QUERIES * QTOK
FEAT = DA + FW
CHIPS = 8
CORES = 2
HOPS = CHIPS // 2
PAD = 16
ROWS = QROWS // (CHIPS * CORES)
IN_HALF, OUT_HALF = DA // CORES, FW // CORES
HALF = IN_HALF + OUT_HALF
IN_CHUNK, OUT_CHUNK = IN_HALF // CHIPS, OUT_HALF // CHIPS
CHUNK = IN_CHUNK + OUT_CHUNK
KTILE = 1024

damping = 0.1
F32 = jnp.float32
BF16 = jnp.bfloat16


def nt(a, b):
    return lax.dot_general(a, b, (((1,), (1,)), ((), ())), preferred_element_type=F32)


def kernel(
    query, basis_in, basis_out, eig_in, eig_out, trace_in, trace_grad, out,
    b_in, b_out, gathered, rot_in_f, rot_out_f, rot_in, rot_out, traces, own,
    sib_recv, ring_send, ring_recv, pair, pair_recv,
    load_sem, q_send, q_recv, qs_send, qs_recv, t_send, t_recv,
    s_send, s_recv, r_send, r_recv, g_send, g_recv, p_send, p_recv,
):
    me = lax.axis_index("basis")
    core = lax.rem(me, 2)
    other = 1 - core
    chip = me // 2
    depth = CHIPS // 2
    pos = jnp.where(lax.rem(chip, 2) == 0, chip // 2, CHIPS - 1 - chip // 2)

    def at(offset):
        return lax.rem(pos + offset + CHIPS, CHIPS)

    def device(place, which):
        spot = jnp.where(place < depth, 2 * place, 2 * (CHIPS - 1 - place) + 1)
        return spot * 2 + which

    sibling = device(pos, other)
    ahead, behind = device(at(1), core), device(at(-1), core)
    toward = (ahead, behind)

    local = [
        pltpu.make_async_copy(basis_in, b_in, load_sem.at[0]),
        pltpu.make_async_copy(basis_out, b_out, load_sem.at[1]),
    ]
    mine = pl.ds(pl.multiple_of(me * PAD, PAD), PAD)
    first = pltpu.make_async_copy(query, gathered.at[mine], load_sem.at[4])
    first.start()

    barrier = pltpu.get_barrier_semaphore()
    for partner in (sibling, ahead, behind):
        pl.semaphore_signal(
            barrier, inc=1, device_id={"basis": partner}, device_id_type=pl.DeviceIdType.MESH
        )
    pl.semaphore_wait(barrier, 3)

    def remote(src, dst, send, recv, target):
        return pltpu.make_async_remote_copy(
            src_ref=src, dst_ref=dst, send_sem=send, recv_sem=recv,
            device_id={"basis": target}, device_id_type=pl.DeviceIdType.MESH,
        )

    first.wait()

    def block(owner, piece):
        rows = pl.ds(pl.multiple_of(owner * PAD, PAD), PAD)
        return gathered.at[rows, pl.ds(piece * HALF, HALF)]

    def hop(way, step, piece):
        owner = device(at(-step if way == 0 else step), core)
        ref = block(owner, piece)
        return remote(
            ref, ref, q_send.at[way, step, piece], q_recv.at[way, step, piece], toward[way]
        )

    def share(slot, place, piece):
        ref = block(device(place, core), piece)
        return remote(ref, ref, qs_send.at[slot, piece], qs_recv.at[slot, piece], sibling)

    q_copies, s_copies = [], []

    def send_query(way, step, piece):
        if step == HOPS - 1 and piece != way:
            return
        copy = hop(way, step, piece)
        copy.start()
        q_copies.append(copy)

    def send_share(slot, place, piece):
        copy = share(slot, place, piece)
        copy.start()
        s_copies.append(copy)

    for piece in range(2):
        for way in range(2):
            send_query(way, 0, (piece + way) % 2)
    for piece in range(2):
        send_share(0, pos, piece)
    for copy in local:
        copy.start()

    def trace_parts(which, target_rows):
        in_from = pl.ds(pl.multiple_of(which * IN_HALF, 128), IN_HALF)
        out_from = pl.ds(pl.multiple_of(which * OUT_HALF, 128), OUT_HALF)
        return (
            (trace_in.at[:, in_from], traces.at[target_rows, pl.ds(0, IN_HALF)]),
            (trace_grad.at[:, out_from], traces.at[target_rows, pl.ds(IN_HALF, OUT_HALF)]),
        )

    local_rows = trace_in.shape[0]
    t_rows = pl.ds(pl.multiple_of(core * local_rows, local_rows), local_rows)
    keep = [
        pltpu.make_async_copy(src, dst, load_sem.at[2 + i])
        for i, (src, dst) in enumerate(trace_parts(core, t_rows))
    ]
    give = [
        remote(src, dst, t_send.at[i], t_recv.at[i], sibling)
        for i, (src, dst) in enumerate(trace_parts(other, t_rows))
    ]

    for step in range(HOPS):
        for piece in range(2):
            for way in range(2):
                part = (piece + way) % 2
                if step == HOPS - 1 and part != way:
                    continue
                hop(way, step, part).wait_recv()
                if step < HOPS - 1:
                    send_query(way, step + 1, part)
                place = at(-1 - step if way == 0 else 1 + step)
                if step == HOPS - 1:
                    send_share(2 * HOPS - 1, place, part)
                else:
                    send_share(1 + 2 * step + way, place, part)
        if step == 0:
            for copy in keep + give:
                copy.start()
    for copy in local:
        copy.wait()
    for copy in s_copies:
        copy.wait()
    for copy in q_copies:
        copy.wait_send()

    rot_in_f[...] = jnp.zeros_like(rot_in_f)
    rot_out_f[...] = jnp.zeros_like(rot_out_f)

    @pl.loop(0, DA // KTILE)
    def _(k):
        start = pl.multiple_of(k * KTILE, KTILE)
        rot_in_f[...] += jnp.dot(
            gathered[:, pl.ds(start, KTILE)], b_in[pl.ds(start, KTILE), :],
            preferred_element_type=F32,
        )

    @pl.loop(0, FW // KTILE)
    def _(k):
        start = pl.multiple_of(k * KTILE, KTILE)
        rot_out_f[...] += jnp.dot(
            gathered[:, pl.ds(start + DA, KTILE)], b_out[pl.ds(start, KTILE), :],
            preferred_element_type=F32,
        )

    for total, eig, rot in ((rot_in_f, eig_in, rot_in), (rot_out_f, eig_out, rot_out)):
        scale = eig[...] + damping
        for i in range(CHIPS * CORES):
            total[pl.ds(i * ROWS, ROWS), :] = total[pl.ds(i * PAD, ROWS), :] / scale
        rot[...] = total[pl.ds(0, QROWS), :].astype(BF16)

    order = [HOPS]
    for d in range(HOPS - 1, 0, -1):
        order += [d, -d]
    order += [0]

    def in_rows(which, place):
        return pl.ds(pl.multiple_of(which * IN_HALF + place * IN_CHUNK, 128), IN_CHUNK)

    def out_rows(which, place):
        return pl.ds(pl.multiple_of(which * OUT_HALF + place * OUT_CHUNK, 128), OUT_CHUNK)

    def stage(j):
        return gathered.at[pl.ds(0, QROWS), pl.ds(HALF + j * CHUNK, CHUNK)]

    sib = []

    def compute(j):
        place = at(order[j])
        stage(j)[:, :IN_CHUNK] = nt(rot_in[...], b_in[in_rows(other, place), :]).astype(BF16)
        stage(j)[:, IN_CHUNK:] = nt(rot_out[...], b_out[out_rows(other, place), :]).astype(BF16)
        copy = remote(stage(j), sib_recv.at[j], s_send.at[j], s_recv.at[j], sibling)
        copy.start()
        sib.append(copy)
        own[j % 3, :, :IN_CHUNK] = nt(rot_in[...], b_in[in_rows(core, place), :])
        own[j % 3, :, IN_CHUNK:] = nt(rot_out[...], b_out[out_rows(core, place), :])

    ring = {}

    def ring_copy(way, step):
        if step == 0:
            rows = pl.ds(way * (QROWS // 2), QROWS // 2)
            src, dst = ring_send.at[way, step, rows], ring_recv.at[way, step, rows]
        else:
            src, dst = ring_send.at[way, step], ring_recv.at[way, step]
        return remote(src, dst, r_send.at[way, step], r_recv.at[way, step], toward[way])

    halves = (pl.ds(0, QROWS // 2), pl.ds(QROWS // 2, QROWS // 2))
    compute(0)
    compute(1)
    compute(2)
    sib[0].wait_recv()
    for way in range(2):
        rows = halves[way]
        ring_send[way, 0, rows] = (own[0, rows] + sib_recv[0, rows].astype(F32)).astype(BF16)
        ring[way, 0] = ring_copy(way, 0)
        ring[way, 0].start()
    for step in range(1, HOPS):
        for way in range(2):
            j = 1 + 2 * (step - 1) + way
            sib[j].wait_recv()
            ring[way, step - 1].wait_recv()
            if step == 1:
                a, b = halves[way], halves[1 - way]
                ring_send[way, 1, a] = (
                    own[j % 3, a] + sib_recv[j, a].astype(F32) + ring_recv[way, 0, a].astype(F32)
                ).astype(BF16)
                ring_send[way, 1, b] = (own[j % 3, b] + sib_recv[j, b].astype(F32)).astype(BF16)
            else:
                ring_send[way, step] = (
                    own[j % 3] + sib_recv[j].astype(F32) + ring_recv[way, step - 1].astype(F32)
                ).astype(BF16)
            ring[way, step] = ring_copy(way, step)
            ring[way, step].start()
        if step < HOPS - 1:
            compute(2 * step + 1)
            compute(2 * step + 2)
        else:
            compute(2 * HOPS - 1)
    last = 2 * HOPS - 1
    sib[last].wait_recv()
    for way in range(2):
        ring[way, HOPS - 1].wait_recv()

    def chunk(place):
        cols = pl.ds(pl.multiple_of(place * CHUNK, 128), CHUNK)
        return gathered.at[pl.ds(0, QROWS), cols]

    chunk(pos)[...] = (
        own[last % 3] + sib_recv[last].astype(F32)
        + ring_recv[0, HOPS - 1].astype(F32) + ring_recv[1, HOPS - 1].astype(F32)
    ).astype(BF16)

    spread = {}

    def spread_copy(way, step):
        place = at(-step if way == 0 else step)
        if step == HOPS - 1:
            rows = halves[way]
            cols = pl.ds(pl.multiple_of(place * CHUNK, 128), CHUNK)
            ref = gathered.at[rows, cols]
        else:
            ref = chunk(place)
        return remote(ref, ref, g_send.at[way, step], g_recv.at[way, step], toward[way])

    for way in range(2):
        spread[way, 0] = spread_copy(way, 0)
        spread[way, 0].start()
    for copy in keep:
        copy.wait()
    for copy in give:
        copy.wait()

    def multiply(place):
        block_of = chunk(place)
        t_in = pl.ds(pl.multiple_of(place * IN_CHUNK, 128), IN_CHUNK)
        t_out = pl.ds(pl.multiple_of(IN_HALF + place * OUT_CHUNK, 128), OUT_CHUNK)
        return (
            nt(traces[:, t_in], block_of[:, :IN_CHUNK]),
            nt(traces[:, t_out], block_of[:, IN_CHUNK:]),
        )

    pair[0], pair[1] = multiply(pos)
    for step in range(HOPS):
        for way in range(2):
            spread[way, step].wait_recv()
            if step < HOPS - 1:
                spread[way, step + 1] = spread_copy(way, step + 1)
                spread[way, step + 1].start()
        for way in range(2 if step < HOPS - 1 else 1):
            a, b = multiply(at(-1 - step if way == 0 else 1 + step))
            pair[0] += a
            pair[1] += b

    their_rows = pl.ds(pl.multiple_of(other * local_rows, local_rows), local_rows)
    swap = remote(pair.at[:, their_rows], pair_recv, p_send, p_recv, sibling)
    swap.start()
    swap.wait_recv()
    left = pair[0, t_rows, :] + pair_recv[0]
    right = pair[1, t_rows, :] + pair_recv[1]
    traces_here = local_rows // TTOK
    products = left * right
    sums = jnp.concatenate(
        [
            jnp.sum(products[i * TTOK : (i + 1) * TTOK], axis=0, keepdims=True)
            for i in range(traces_here)
        ],
        axis=0,
    )
    query_of = lax.broadcasted_iota(jnp.int32, (QUERIES, QROWS), 0) * QTOK
    token = lax.broadcasted_iota(jnp.int32, (QUERIES, QROWS), 1)
    select = jnp.where((token >= query_of) & (token < query_of + QTOK), 1.0, 0.0).astype(F32)
    scores = lax.dot_general(
        select, sums, (((1,), (1,)), ((), ())),
        precision=lax.Precision.HIGHEST, preferred_element_type=F32,
    )
    out[...] = scores * (1.0 / (math.sqrt(DA) * math.sqrt(FW) * TTOK * QTOK))

    swap.wait_send()
    for copy in sib:
        copy.wait_send()
    for copy in list(ring.values()) + list(spread.values()):
        copy.wait_send()


def per_device_ring(
    query_inputs, query_grads, basis_in, basis_out, eig_in, eig_out, trace_inputs, trace_grads
):
    query = jnp.pad(
        jnp.concatenate([query_inputs, query_grads], axis=1), ((0, PAD - ROWS), (0, 0))
    )
    cin, cout = basis_in.shape[1], basis_out.shape[1]
    rows = trace_inputs.shape[0]
    dma = pltpu.SemaphoreType.DMA
    padded = CHIPS * CORES * PAD
    vmem = pl.BlockSpec(memory_space=pltpu.VMEM)
    hbm = pl.BlockSpec(memory_space=pl.ANY)
    return pl.pallas_call(
        kernel,
        out_shape=jax.ShapeDtypeStruct((QUERIES, rows // TTOK), F32),
        in_specs=[hbm, hbm, hbm, vmem, vmem, hbm, hbm],
        out_specs=vmem,
        scratch_shapes=[
            pltpu.VMEM((DA, cin), BF16),
            pltpu.VMEM((FW, cout), BF16),
            pltpu.VMEM((padded, FEAT), BF16),
            pltpu.VMEM((padded, cin), F32),
            pltpu.VMEM((padded, cout), F32),
            pltpu.VMEM((QROWS, cin), BF16),
            pltpu.VMEM((QROWS, cout), BF16),
            pltpu.VMEM((CORES * rows, HALF), BF16),
            pltpu.VMEM((3, QROWS, CHUNK), F32),
            pltpu.VMEM((2 * HOPS, QROWS, CHUNK), BF16),
            pltpu.VMEM((2, HOPS, QROWS, CHUNK), BF16),
            pltpu.VMEM((2, HOPS, QROWS, CHUNK), BF16),
            pltpu.VMEM((2, CORES * rows, QROWS), F32),
            pltpu.VMEM((2, rows, QROWS), F32),
            dma((5,)),
            dma((2, HOPS, 2)),
            dma((2, HOPS, 2)),
            dma((2 * HOPS, 2)),
            dma((2 * HOPS, 2)),
            dma((2,)),
            dma((2,)),
            dma((2 * HOPS,)),
            dma((2 * HOPS,)),
            dma((2, HOPS)),
            dma((2, HOPS)),
            dma((2, HOPS)),
            dma((2, HOPS)),
            dma(()),
            dma(()),
        ],
        compiler_params=pltpu.CompilerParams(
            collective_id=0, has_side_effects=True, vmem_limit_bytes=63 * 1024 * 1024
        ),
        name="influence",
    )(
        query, basis_in, basis_out, eig_in.reshape(1, cin), eig_out.reshape(1, cout),
        trace_inputs, trace_grads,
    )


def per_device_plain(
    query_inputs, query_grads, basis_in, basis_out, eig_in, eig_out, trace_inputs, trace_grads
):
    def gather(x):
        return lax.all_gather(x, "basis", axis=0, tiled=True)

    def condition(query, basis, eig):
        rot = (jnp.dot(gather(query), basis, preferred_element_type=F32) / (eig + damping)).astype(
            BF16
        )
        share = lax.psum_scatter(
            jnp.dot(basis, rot.T, preferred_element_type=F32),
            "basis",
            scatter_dimension=0,
            tiled=True,
        )
        return gather(share.astype(BF16)).astype(F32)

    pre_in = condition(query_inputs, basis_in, eig_in)
    pre_grad = condition(query_grads, basis_out, eig_out)
    high = lax.Precision.HIGHEST
    pair_in = jnp.dot(trace_inputs.astype(F32), pre_in, precision=high) / math.sqrt(DA)
    pair_grad = jnp.dot(trace_grads.astype(F32), pre_grad, precision=high) / math.sqrt(FW)
    local_traces = trace_inputs.shape[0] // TTOK
    products = (pair_in * pair_grad).reshape(local_traces, TTOK, QUERIES, QTOK)
    return jnp.sum(products, axis=(1, 3)).T / (TTOK * QTOK)


def solution(mesh):
    fits = mesh.shape["basis"] == CHIPS * CORES
    return jax.shard_map(
        per_device_ring if fits else per_device_plain,
        mesh=mesh,
        in_specs=(
            P(("grp", "basis"), None),
            P(("grp", "basis"), None),
            P(None, "basis"),
            P(None, "basis"),
            P("basis"),
            P("basis"),
            P(("grp", "basis"), None),
            P(("grp", "basis"), None),
        ),
        out_specs=P(None, ("grp", "basis")),
        check_vma=False,
    )
```

```python
import functools
import math

import jax
import jax.numpy as jnp
from jax import lax
from jax.experimental import pallas as pl
from jax.experimental.pallas import tpu as pltpu
from jax.sharding import PartitionSpec as P

DA = 4096
FW = 14336
QUERIES = 64
QTOK = 3
TTOK = 64
QROWS = QUERIES * QTOK
FEAT = DA + FW
CHIPS = 8
CORES = 2
HOPS = CHIPS // 2
PAD = 16
ROWS = QROWS // (CHIPS * CORES)
IN_HALF, OUT_HALF = DA // CORES, FW // CORES
HALF = IN_HALF + OUT_HALF
IN_CHUNK, OUT_CHUNK = IN_HALF // CHIPS, OUT_HALF // CHIPS
CHUNK = IN_CHUNK + OUT_CHUNK
KTILE = 1024
GROUPS = 3
SPARE = PAD - ROWS
EXTRA = FEAT // (GROUPS + 1)
WIDE = FEAT - EXTRA
PARTS = ((0, GROUPS - 1), (GROUPS - 1, GROUPS))
TAIL = FW - EXTRA
ETILE = EXTRA // 3

damping = 0.1
F32 = jnp.float32
BF16 = jnp.bfloat16


def nt(a, b):
    return lax.dot_general(a, b, (((1,), (1,)), ((), ())), preferred_element_type=F32)


def kernel(
    query, basis_in, basis_out, eig_in, eig_out, trace_in, trace_grad, out,
    b_in, b_out, gathered, extra, lifted, rot_in_f, rot_out_f, rot_extra, rot_in, rot_out,
    traces, own,
    sib_recv, ring_send, ring_recv, pair, pair_recv,
    load_sem, q_send, q_recv, qs_send, qs_recv, t_send, t_recv,
    s_send, s_recv, r_send, r_recv, g_send, g_recv, p_send, p_recv,
):
    me = lax.axis_index("basis")
    core = lax.rem(me, 2)
    other = 1 - core
    chip = me // 2
    depth = CHIPS // 2
    pos = jnp.where(lax.rem(chip, 2) == 0, chip // 2, CHIPS - 1 - chip // 2)

    def at(offset):
        return lax.rem(pos + offset + CHIPS, CHIPS)

    def device(place, which):
        spot = jnp.where(place < depth, 2 * place, 2 * (CHIPS - 1 - place) + 1)
        return spot * 2 + which

    sibling = device(pos, other)
    ahead, behind = device(at(1), core), device(at(-1), core)
    toward = (ahead, behind)

    local = [
        pltpu.make_async_copy(basis_in, b_in, load_sem.at[0]),
        pltpu.make_async_copy(basis_out, b_out, load_sem.at[1]),
    ]
    mine = pl.ds(pl.multiple_of(me * PAD, PAD), PAD)
    first = pltpu.make_async_copy(query, gathered.at[mine], load_sem.at[4])
    first.start()

    barrier = pltpu.get_barrier_semaphore()
    for partner in (sibling, ahead, behind):
        pl.semaphore_signal(
            barrier, inc=1, device_id={"basis": partner}, device_id_type=pl.DeviceIdType.MESH
        )
    pl.semaphore_wait(barrier, 3)

    def remote(src, dst, send, recv, target):
        return pltpu.make_async_remote_copy(
            src_ref=src, dst_ref=dst, send_sem=send, recv_sem=recv,
            device_id={"basis": target}, device_id_type=pl.DeviceIdType.MESH,
        )

    first.wait()

    def block(owner, part, piece):
        rows = pl.ds(pl.multiple_of(owner * PAD, PAD), PAD)
        low, high = PARTS[part]
        width = (high - low) * EXTRA // 2
        return gathered.at[rows, pl.ds(low * EXTRA + piece * width, width)]

    def hop(part, way, step, piece):
        owner = device(at(-step if way == 0 else step), core)
        ref = block(owner, part, piece)
        sems = q_send.at[part, way, step, piece], q_recv.at[part, way, step, piece]
        return remote(ref, ref, *sems, toward[way])

    q_copies, s_copies = [], ([], [])

    def send_query(part, way, step, piece):
        if step == HOPS - 1 and piece != way:
            return
        copy = hop(part, way, step, piece)
        copy.start()
        q_copies.append(copy)

    def send_share(part, slot, place, piece):
        ref = block(device(place, core), part, piece)
        sems = qs_send.at[part, slot, piece], qs_recv.at[part, slot, piece]
        copy = remote(ref, ref, *sems, sibling)
        copy.start()
        s_copies[part].append(copy)

    def open_part(part):
        for piece in range(2):
            for way in range(2):
                send_query(part, way, 0, (piece + way) % 2)
        for piece in range(2):
            send_share(part, 0, pos, piece)

    def pass_on(part, step, turn):
        for way in range(2):
            piece = (turn + way) % 2
            if step == HOPS - 1 and piece != way:
                continue
            hop(part, way, step, piece).wait_recv()
            if step < HOPS - 1:
                send_query(part, way, step + 1, piece)
            place = at(-1 - step if way == 0 else 1 + step)
            slot = 2 * HOPS - 1 if step == HOPS - 1 else 1 + 2 * step + way
            send_share(part, slot, place, piece)

    open_part(0)
    for copy in local:
        copy.start()

    def trace_parts(which, target_rows):
        in_from = pl.ds(pl.multiple_of(which * IN_HALF, 128), IN_HALF)
        out_from = pl.ds(pl.multiple_of(which * OUT_HALF, 128), OUT_HALF)
        return (
            (trace_in.at[:, in_from], traces.at[target_rows, pl.ds(0, IN_HALF)]),
            (trace_grad.at[:, out_from], traces.at[target_rows, pl.ds(IN_HALF, OUT_HALF)]),
        )

    local_rows = trace_in.shape[0]
    t_rows = pl.ds(pl.multiple_of(core * local_rows, local_rows), local_rows)
    keep = [
        pltpu.make_async_copy(src, dst, load_sem.at[2 + i])
        for i, (src, dst) in enumerate(trace_parts(core, t_rows))
    ]
    give = [
        remote(src, dst, t_send.at[i], t_recv.at[i], sibling)
        for i, (src, dst) in enumerate(trace_parts(other, t_rows))
    ]

    rounds = [(step, turn) for step in range(HOPS) for turn in range(2)][: 2 * HOPS - 1]
    for i, (step, turn) in enumerate(rounds):
        if i == len(rounds) - 1:
            open_part(1)
        pass_on(0, step, turn)
        if i == 1:
            for copy in keep + give:
                copy.start()

    def add_in(start):
        rot_in_f[...] += jnp.dot(
            gathered[:, start : start + KTILE], b_in[start : start + KTILE, :],
            preferred_element_type=F32,
        )

    def add_out(start, size):
        rot_out_f[...] += jnp.dot(
            gathered[:, start + DA : start + DA + size], b_out[start : start + size, :],
            preferred_element_type=F32,
        )

    def lift(group):
        cols = pl.ds(group * EXTRA, EXTRA)
        per_tile = PAD // SPARE
        tiles = CHIPS * CORES // per_tile
        for tile in range(tiles):
            for i in range(per_tile):
                rows = pl.ds((tile * per_tile + i) * PAD, PAD)
                lifted[pl.ds(i * SPARE, SPARE), :] = gathered[rows, cols].astype(F32)[ROWS:]
            extra[pl.ds((group * tiles + tile) * PAD, PAD), :] = lifted[...].astype(BF16)

    block_rows = CHIPS * CORES * SPARE

    def add_extra(part, start):
        low, high = PARTS[part]
        rows = pl.ds(low * block_rows, (high - low) * block_rows)
        rot_extra[rows, :] += jnp.dot(
            extra[rows, start : start + ETILE],
            b_out[TAIL + start : TAIL + start + ETILE, :],
            preferred_element_type=F32,
        )

    early = PARTS[0][1] * EXTRA - DA
    rot_in_f[...] = jnp.zeros_like(rot_in_f)
    rot_out_f[...] = jnp.zeros_like(rot_out_f)
    rot_extra[...] = jnp.zeros_like(rot_extra)
    jobs = [functools.partial(add_in, k) for k in range(0, DA, KTILE)]
    jobs += [functools.partial(add_out, k, KTILE) for k in range(0, early, KTILE)]
    jobs += [functools.partial(lift, g) for g in range(*PARTS[0])]
    jobs += [functools.partial(add_extra, 0, k) for k in range(0, EXTRA, ETILE)]
    share_out = -(-len(jobs) // (len(rounds) - 1))
    for i, (step, turn) in enumerate(rounds):
        pass_on(1, step, turn)
        if i == 0:
            for copy in local:
                copy.wait()
            for copy in s_copies[0]:
                copy.wait()
        for job in jobs[i * share_out : (i + 1) * share_out]:
            job()
    for copy in s_copies[1]:
        copy.wait()
    for group in range(*PARTS[1]):
        lift(group)
    for k in range(early, TAIL, ETILE):
        add_out(k, ETILE)
    for k in range(0, EXTRA, ETILE):
        add_extra(1, k)
    for copy in q_copies:
        copy.wait_send()

    scale = eig_in[...] + damping
    for i in range(CHIPS * CORES):
        rot_in_f[pl.ds(i * ROWS, ROWS), :] = rot_in_f[pl.ds(i * PAD, ROWS), :] / scale
    rot_in[...] = rot_in_f[pl.ds(0, QROWS), :].astype(BF16)
    scale = eig_out[...] + damping
    for i in range(CHIPS * CORES):
        for group in range(GROUPS):
            rot_out_f[pl.ds(i * ROWS + group * SPARE, SPARE), :] = (
                rot_out_f[pl.ds(i * PAD + group * SPARE, SPARE), :]
                + rot_extra[pl.ds(group * block_rows + i * SPARE, SPARE), :]
            ) / scale
    rot_out[...] = rot_out_f[pl.ds(0, QROWS), :].astype(BF16)

    order = [HOPS]
    for d in range(HOPS - 1, 0, -1):
        order += [d, -d]
    order += [0]

    def in_rows(which, place):
        return pl.ds(pl.multiple_of(which * IN_HALF + place * IN_CHUNK, 128), IN_CHUNK)

    def out_rows(which, place):
        return pl.ds(pl.multiple_of(which * OUT_HALF + place * OUT_CHUNK, 128), OUT_CHUNK)

    def stage(j):
        spots = (WIDE - HALF) // CHUNK
        if j < spots:
            return gathered.at[pl.ds(0, QROWS), pl.ds(HALF + j * CHUNK, CHUNK)]
        return extra.at[:, pl.ds((j - spots) * CHUNK, CHUNK)]

    sib = []

    def compute(j):
        place = at(order[j])
        stage(j)[:, :IN_CHUNK] = nt(rot_in[...], b_in[in_rows(other, place), :]).astype(BF16)
        stage(j)[:, IN_CHUNK:] = nt(rot_out[...], b_out[out_rows(other, place), :]).astype(BF16)
        copy = remote(stage(j), sib_recv.at[j], s_send.at[j], s_recv.at[j], sibling)
        copy.start()
        sib.append(copy)
        own[j % 3, :, :IN_CHUNK] = nt(rot_in[...], b_in[in_rows(core, place), :])
        own[j % 3, :, IN_CHUNK:] = nt(rot_out[...], b_out[out_rows(core, place), :])

    ring = {}
    halves = (pl.ds(0, QROWS // 2), pl.ds(QROWS // 2, QROWS // 2))

    def send_sum(step, far):
        for way in range(2):
            half = way if far else 1 - way
            rows = halves[half]
            j = 0 if step == 0 else 2 * step - 1 + way
            if ("sib", j) not in seen:
                sib[j].wait_recv()
                seen.add(("sib", j))
            total = own[j % 3, rows] + sib_recv[j, rows].astype(F32)
            if (way, step - 1, half) in ring:
                ring[way, step - 1, half].wait_recv()
                total = total + ring_recv[way, step - 1, rows].astype(F32)
            ring_send[way, step, rows] = total.astype(BF16)
            copy = remote(
                ring_send.at[way, step, rows], ring_recv.at[way, step, rows],
                r_send.at[way, step, half], r_recv.at[way, step, half], toward[way],
            )
            copy.start()
            ring[way, step, half] = copy

    seen = set()
    compute(0)
    send_sum(0, True)
    compute(1)
    compute(2)
    for step in range(1, HOPS):
        send_sum(step, False)
        compute(2 * step + 1)
        send_sum(step, True)
        if step < HOPS - 1:
            compute(2 * step + 2)
    last = 2 * HOPS - 1
    sib[last].wait_recv()

    def chunk(place):
        cols = pl.ds(pl.multiple_of(place * CHUNK, 128), CHUNK)
        return gathered.at[pl.ds(0, QROWS), cols]

    spread = {}

    def part_of(place, half):
        cols = pl.ds(pl.multiple_of(place * CHUNK, 128), CHUNK)
        return gathered.at[halves[half], cols]

    def send_spread(way, step, half):
        if step == HOPS - 1 and half != way:
            return
        ref = part_of(at(-step if way == 0 else step), half)
        sems = g_send.at[way, step, half], g_recv.at[way, step, half]
        copy = remote(ref, ref, *sems, toward[way])
        copy.start()
        spread[way, step, half] = copy

    for half in (1, 0):
        ring[half ^ 1, HOPS - 1, half].wait_recv()
    for half in range(2):
        ring[half, HOPS - 1, half].wait_recv()
        rows = halves[half]
        part_of(pos, half)[...] = (
            own[last % 3, rows] + sib_recv[last, rows].astype(F32)
            + ring_recv[0, HOPS - 1, rows].astype(F32)
            + ring_recv[1, HOPS - 1, rows].astype(F32)
        ).astype(BF16)
    for turn in range(2):
        for way in range(2):
            send_spread(way, 0, (turn + way) % 2)
    for copy in keep:
        copy.wait()
    for copy in give:
        copy.wait()

    def multiply(place):
        block_of = chunk(place)
        t_in = pl.ds(pl.multiple_of(place * IN_CHUNK, 128), IN_CHUNK)
        t_out = pl.ds(pl.multiple_of(IN_HALF + place * OUT_CHUNK, 128), OUT_CHUNK)
        return (
            nt(traces[:, t_in], block_of[:, :IN_CHUNK]),
            nt(traces[:, t_out], block_of[:, IN_CHUNK:]),
        )

    pair[0], pair[1] = multiply(pos)
    for step in range(HOPS):
        for turn in range(2):
            for way in range(2):
                half = (turn + way) % 2
                if (way, step, half) in spread:
                    spread[way, step, half].wait_recv()
                    if step < HOPS - 1:
                        send_spread(way, step + 1, half)
        for way in range(2 if step < HOPS - 1 else 1):
            a, b = multiply(at(-1 - step if way == 0 else 1 + step))
            pair[0] += a
            pair[1] += b

    their_rows = pl.ds(pl.multiple_of(other * local_rows, local_rows), local_rows)
    swap = remote(pair.at[:, their_rows], pair_recv, p_send, p_recv, sibling)
    swap.start()
    swap.wait_recv()
    left = pair[0, t_rows, :] + pair_recv[0]
    right = pair[1, t_rows, :] + pair_recv[1]
    traces_here = local_rows // TTOK
    products = left * right
    sums = jnp.concatenate(
        [
            jnp.sum(products[i * TTOK : (i + 1) * TTOK], axis=0, keepdims=True)
            for i in range(traces_here)
        ],
        axis=0,
    )
    query_of = lax.broadcasted_iota(jnp.int32, (QUERIES, QROWS), 0) * QTOK
    token = lax.broadcasted_iota(jnp.int32, (QUERIES, QROWS), 1)
    select = jnp.where((token >= query_of) & (token < query_of + QTOK), 1.0, 0.0).astype(F32)
    scores = lax.dot_general(
        select, sums, (((1,), (1,)), ((), ())),
        precision=lax.Precision.HIGHEST, preferred_element_type=F32,
    )
    out[...] = scores * (1.0 / (math.sqrt(DA) * math.sqrt(FW) * TTOK * QTOK))

    swap.wait_send()
    for copy in sib:
        copy.wait_send()
    for copy in list(ring.values()) + list(spread.values()):
        copy.wait_send()


def per_device_ring(
    query_inputs, query_grads, basis_in, basis_out, eig_in, eig_out, trace_inputs, trace_grads
):
    spare = query_grads[:, TAIL:].reshape(GROUPS, SPARE, EXTRA).swapaxes(0, 1)
    query = jnp.concatenate(
        [
            jnp.concatenate([query_inputs, query_grads[:, :TAIL]], axis=1),
            spare.reshape(SPARE, WIDE),
        ],
        axis=0,
    )
    cin, cout = basis_in.shape[1], basis_out.shape[1]
    rows = trace_inputs.shape[0]
    dma = pltpu.SemaphoreType.DMA
    padded = CHIPS * CORES * PAD
    vmem = pl.BlockSpec(memory_space=pltpu.VMEM)
    hbm = pl.BlockSpec(memory_space=pl.ANY)
    return pl.pallas_call(
        kernel,
        out_shape=jax.ShapeDtypeStruct((QUERIES, rows // TTOK), F32),
        in_specs=[hbm, hbm, hbm, vmem, vmem, hbm, hbm],
        out_specs=vmem,
        scratch_shapes=[
            pltpu.VMEM((DA, cin), BF16),
            pltpu.VMEM((FW, cout), BF16),
            pltpu.VMEM((padded, WIDE), BF16),
            pltpu.VMEM((QROWS, EXTRA), BF16),
            pltpu.VMEM((PAD, EXTRA), F32),
            pltpu.VMEM((padded, cin), F32),
            pltpu.VMEM((padded, cout), F32),
            pltpu.VMEM((QROWS, cout), F32),
            pltpu.VMEM((QROWS, cin), BF16),
            pltpu.VMEM((QROWS, cout), BF16),
            pltpu.VMEM((CORES * rows, HALF), BF16),
            pltpu.VMEM((3, QROWS, CHUNK), F32),
            pltpu.VMEM((2 * HOPS, QROWS, CHUNK), BF16),
            pltpu.VMEM((2, HOPS, QROWS, CHUNK), BF16),
            pltpu.VMEM((2, HOPS, QROWS, CHUNK), BF16),
            pltpu.VMEM((2, CORES * rows, QROWS), F32),
            pltpu.VMEM((2, rows, QROWS), F32),
            dma((5,)),
            dma((2, 2, HOPS, 2)),
            dma((2, 2, HOPS, 2)),
            dma((2, 2 * HOPS, 2)),
            dma((2, 2 * HOPS, 2)),
            dma((2,)),
            dma((2,)),
            dma((2 * HOPS,)),
            dma((2 * HOPS,)),
            dma((2, HOPS, 2)),
            dma((2, HOPS, 2)),
            dma((2, HOPS, 2)),
            dma((2, HOPS, 2)),
            dma(()),
            dma(()),
        ],
        compiler_params=pltpu.CompilerParams(
            collective_id=0, has_side_effects=True, vmem_limit_bytes=63 * 1024 * 1024
        ),
        name="influence",
    )(
        query, basis_in, basis_out, eig_in.reshape(1, cin), eig_out.reshape(1, cout),
        trace_inputs, trace_grads,
    )


def per_device_plain(
    query_inputs, query_grads, basis_in, basis_out, eig_in, eig_out, trace_inputs, trace_grads
):
    def gather(x):
        return lax.all_gather(x, "basis", axis=0, tiled=True)

    def condition(query, basis, eig):
        rot = (jnp.dot(gather(query), basis, preferred_element_type=F32) / (eig + damping)).astype(
            BF16
        )
        share = lax.psum_scatter(
            jnp.dot(basis, rot.T, preferred_element_type=F32),
            "basis",
            scatter_dimension=0,
            tiled=True,
        )
        return gather(share.astype(BF16)).astype(F32)

    pre_in = condition(query_inputs, basis_in, eig_in)
    pre_grad = condition(query_grads, basis_out, eig_out)
    high = lax.Precision.HIGHEST
    pair_in = jnp.dot(trace_inputs.astype(F32), pre_in, precision=high) / math.sqrt(DA)
    pair_grad = jnp.dot(trace_grads.astype(F32), pre_grad, precision=high) / math.sqrt(FW)
    local_traces = trace_inputs.shape[0] // TTOK
    products = (pair_in * pair_grad).reshape(local_traces, TTOK, QUERIES, QTOK)
    return jnp.sum(products, axis=(1, 3)).T / (TTOK * QTOK)


def solution(mesh):
    fits = mesh.shape["basis"] == CHIPS * CORES
    return jax.shard_map(
        per_device_ring if fits else per_device_plain,
        mesh=mesh,
        in_specs=(
            P(("grp", "basis"), None),
            P(("grp", "basis"), None),
            P(None, "basis"),
            P(None, "basis"),
            P("basis"),
            P("basis"),
            P(("grp", "basis"), None),
            P(("grp", "basis"), None),
        ),
        out_specs=P(None, ("grp", "basis")),
        check_vma=False,
    )
```

```python
import functools
import math

import jax
import jax.numpy as jnp
from jax import lax
from jax.experimental import pallas as pl
from jax.experimental.pallas import tpu as pltpu
from jax.sharding import PartitionSpec as P

DA = 4096
FW = 14336
QUERIES = 64
QTOK = 3
TTOK = 64
QROWS = QUERIES * QTOK
FEAT = DA + FW
CHIPS = 8
CORES = 2
HOPS = CHIPS // 2
PAD = 16
ROWS = QROWS // (CHIPS * CORES)
IN_HALF, OUT_HALF = DA // CORES, FW // CORES
HALF = IN_HALF + OUT_HALF
IN_CHUNK, OUT_CHUNK = IN_HALF // CHIPS, OUT_HALF // CHIPS
CHUNK = IN_CHUNK + OUT_CHUNK
KTILE = 1024
GROUPS = 3
SPARE = PAD - ROWS
EXTRA = FEAT // (GROUPS + 1)
WIDE = FEAT - EXTRA
PARTS = ((0, GROUPS - 1), (GROUPS - 1, GROUPS))
TAIL = FW - EXTRA
ETILE = EXTRA // 3
LEAD = 1

damping = 0.1
F32 = jnp.float32
BF16 = jnp.bfloat16


def nt(a, b):
    return lax.dot_general(a, b, (((1,), (1,)), ((), ())), preferred_element_type=F32)


def kernel(
    query, basis_in, basis_out, eig_in, eig_out, trace_in, trace_grad, out,
    b_in, b_out, gathered, extra, lifted, rot_in_f, rot_out_f, rot_extra, rot_in, rot_out,
    traces, own,
    sib_recv, ring_send, ring_recv, pair, pair_recv,
    load_sem, q_send, q_recv, qs_send, qs_recv, t_send, t_recv,
    s_send, s_recv, r_send, r_recv, g_send, g_recv, p_send, p_recv,
):
    me = lax.axis_index("basis")
    core = lax.rem(me, 2)
    other = 1 - core
    chip = me // 2
    depth = CHIPS // 2
    pos = jnp.where(lax.rem(chip, 2) == 0, chip // 2, CHIPS - 1 - chip // 2)

    def at(offset):
        return lax.rem(pos + offset + CHIPS, CHIPS)

    def device(place, which):
        spot = jnp.where(place < depth, 2 * place, 2 * (CHIPS - 1 - place) + 1)
        return spot * 2 + which

    sibling = device(pos, other)
    ahead, behind = device(at(1), core), device(at(-1), core)
    toward = (ahead, behind)

    local = [
        pltpu.make_async_copy(basis_in, b_in, load_sem.at[0]),
        pltpu.make_async_copy(basis_out, b_out, load_sem.at[1]),
    ]
    mine = pl.ds(pl.multiple_of(me * PAD, PAD), PAD)
    first = pltpu.make_async_copy(query, gathered.at[mine], load_sem.at[4])
    first.start()

    barrier = pltpu.get_barrier_semaphore()
    for partner in (sibling, ahead, behind):
        pl.semaphore_signal(
            barrier, inc=1, device_id={"basis": partner}, device_id_type=pl.DeviceIdType.MESH
        )
    pl.semaphore_wait(barrier, 3)

    def remote(src, dst, send, recv, target):
        return pltpu.make_async_remote_copy(
            src_ref=src, dst_ref=dst, send_sem=send, recv_sem=recv,
            device_id={"basis": target}, device_id_type=pl.DeviceIdType.MESH,
        )

    def block(owner, part, piece):
        rows = pl.ds(pl.multiple_of(owner * PAD, PAD), PAD)
        low, high = PARTS[part]
        width = (high - low) * EXTRA // 2
        return gathered.at[rows, pl.ds(low * EXTRA + piece * width, width)]

    def origin(part, piece):
        low, high = PARTS[part]
        width = (high - low) * EXTRA // 2
        return query.at[:, pl.ds(low * EXTRA + piece * width, width)]

    def hop(part, way, step, piece):
        owner = device(at(-step if way == 0 else step), core)
        ref = block(owner, part, piece)
        src = origin(part, piece) if step == 0 else ref
        sems = q_send.at[part, way, step, piece], q_recv.at[part, way, step, piece]
        return remote(src, ref, *sems, toward[way])

    q_copies, s_copies = [], ([], [])

    def send_query(part, way, step, piece):
        if step == HOPS - 1 and piece != way:
            return
        copy = hop(part, way, step, piece)
        copy.start()
        q_copies.append(copy)

    def send_share(part, slot, place, piece):
        ref = block(device(place, core), part, piece)
        sems = qs_send.at[part, slot, piece], qs_recv.at[part, slot, piece]
        src = origin(part, piece) if slot == 0 else ref
        copy = remote(src, ref, *sems, sibling)
        copy.start()
        s_copies[part].append(copy)

    def open_part(part):
        for piece in range(2):
            for way in range(2):
                send_query(part, way, 0, (piece + way) % 2)
        for piece in range(2):
            send_share(part, 0, pos, piece)

    def pass_on(part, step, turn):
        for way in range(2):
            piece = (turn + way) % 2
            if step == HOPS - 1 and piece != way:
                continue
            hop(part, way, step, piece).wait_recv()
            if step < HOPS - 1:
                send_query(part, way, step + 1, piece)
            place = at(-1 - step if way == 0 else 1 + step)
            slot = 2 * HOPS - 1 if step == HOPS - 1 else 1 + 2 * step + way
            send_share(part, slot, place, piece)

    open_part(0)
    for copy in local:
        copy.start()

    def trace_parts(which, target_rows):
        in_from = pl.ds(pl.multiple_of(which * IN_HALF, 128), IN_HALF)
        out_from = pl.ds(pl.multiple_of(which * OUT_HALF, 128), OUT_HALF)
        return (
            (trace_in.at[:, in_from], traces.at[target_rows, pl.ds(0, IN_HALF)]),
            (trace_grad.at[:, out_from], traces.at[target_rows, pl.ds(IN_HALF, OUT_HALF)]),
        )

    local_rows = trace_in.shape[0]
    t_rows = pl.ds(pl.multiple_of(core * local_rows, local_rows), local_rows)
    keep = [
        pltpu.make_async_copy(src, dst, load_sem.at[2 + i])
        for i, (src, dst) in enumerate(trace_parts(core, t_rows))
    ]
    give = [
        remote(src, dst, t_send.at[i], t_recv.at[i], sibling)
        for i, (src, dst) in enumerate(trace_parts(other, t_rows))
    ]

    rounds = [(step, turn) for step in range(HOPS) for turn in range(2)][: 2 * HOPS - 1]
    for i, (step, turn) in enumerate(rounds):
        if i == len(rounds) - LEAD - 1:
            open_part(1)
        pass_on(0, step, turn)
        if i >= len(rounds) - LEAD:
            pass_on(1, *rounds[i - len(rounds) + LEAD])
        if i == 1:
            for copy in keep + give:
                copy.start()

    def add_in(start):
        rot_in_f[...] += jnp.dot(
            gathered[:, start : start + KTILE], b_in[start : start + KTILE, :],
            preferred_element_type=F32,
        )

    def add_out(start, size):
        rot_out_f[...] += jnp.dot(
            gathered[:, start + DA : start + DA + size], b_out[start : start + size, :],
            preferred_element_type=F32,
        )

    def lift(group):
        cols = pl.ds(group * EXTRA, EXTRA)
        per_tile = PAD // SPARE
        tiles = CHIPS * CORES // per_tile
        for tile in range(tiles):
            for i in range(per_tile):
                rows = pl.ds((tile * per_tile + i) * PAD, PAD)
                lifted[pl.ds(i * SPARE, SPARE), :] = gathered[rows, cols].astype(F32)[ROWS:]
            extra[pl.ds((group * tiles + tile) * PAD, PAD), :] = lifted[...].astype(BF16)

    block_rows = CHIPS * CORES * SPARE

    def add_extra(part, start):
        low, high = PARTS[part]
        rows = pl.ds(low * block_rows, (high - low) * block_rows)
        rot_extra[rows, :] += jnp.dot(
            extra[rows, start : start + ETILE],
            b_out[TAIL + start : TAIL + start + ETILE, :],
            preferred_element_type=F32,
        )

    def finish_in():
        scale = eig_in[...].reshape(1, -1) + damping
        for i in range(CHIPS * CORES):
            rot_in_f[pl.ds(i * ROWS, ROWS), :] = rot_in_f[pl.ds(i * PAD, ROWS), :] / scale
        rot_in[...] = rot_in_f[pl.ds(0, QROWS), :].astype(BF16)

    early = PARTS[0][1] * EXTRA - DA
    rot_in_f[...] = jnp.zeros_like(rot_in_f)
    rot_out_f[...] = jnp.zeros_like(rot_out_f)
    rot_extra[...] = jnp.zeros_like(rot_extra)
    jobs = [functools.partial(add_in, k) for k in range(0, DA, KTILE)]
    jobs += [finish_in]
    jobs += [functools.partial(add_out, k, KTILE) for k in range(0, early, KTILE)]
    jobs += [functools.partial(lift, g) for g in range(*PARTS[0])]
    jobs += [functools.partial(add_extra, 0, k) for k in range(0, EXTRA, ETILE)]
    rest = rounds[LEAD:]
    share_out = -(-len(jobs) // len(rest))
    for i, (step, turn) in enumerate(rest):
        pass_on(1, step, turn)
        if i == 0:
            first.wait()
            for copy in local:
                copy.wait()
            for copy in s_copies[0]:
                copy.wait()
        for job in jobs[i * share_out : (i + 1) * share_out]:
            job()
    for copy in s_copies[1]:
        copy.wait()
    for group in range(*PARTS[1]):
        lift(group)
    for k in range(early, TAIL, ETILE):
        add_out(k, ETILE)
    for k in range(0, EXTRA, ETILE):
        add_extra(1, k)
    for copy in q_copies:
        copy.wait_send()

    scale = eig_out[...].reshape(1, -1) + damping
    for i in range(CHIPS * CORES):
        for group in range(GROUPS):
            rot_out_f[pl.ds(i * ROWS + group * SPARE, SPARE), :] = (
                rot_out_f[pl.ds(i * PAD + group * SPARE, SPARE), :]
                + rot_extra[pl.ds(group * block_rows + i * SPARE, SPARE), :]
            ) / scale
    rot_out[...] = rot_out_f[pl.ds(0, QROWS), :].astype(BF16)

    order = [HOPS]
    for d in range(HOPS - 1, 0, -1):
        order += [d, -d]
    order += [0]

    def in_rows(which, place):
        return pl.ds(pl.multiple_of(which * IN_HALF + place * IN_CHUNK, 128), IN_CHUNK)

    def out_rows(which, place):
        return pl.ds(pl.multiple_of(which * OUT_HALF + place * OUT_CHUNK, 128), OUT_CHUNK)

    def stage(j):
        spots = (WIDE - HALF) // CHUNK
        if j < spots:
            return gathered.at[pl.ds(0, QROWS), pl.ds(HALF + j * CHUNK, CHUNK)]
        return extra.at[:, pl.ds((j - spots) * CHUNK, CHUNK)]

    sib = []

    def compute(j):
        place = at(order[j])
        stage(j)[:, :IN_CHUNK] = nt(rot_in[...], b_in[in_rows(other, place), :]).astype(BF16)
        stage(j)[:, IN_CHUNK:] = nt(rot_out[...], b_out[out_rows(other, place), :]).astype(BF16)
        copy = remote(stage(j), sib_recv.at[j], s_send.at[j], s_recv.at[j], sibling)
        copy.start()
        sib.append(copy)
        own[j % 3, :, :IN_CHUNK] = nt(rot_in[...], b_in[in_rows(core, place), :])
        own[j % 3, :, IN_CHUNK:] = nt(rot_out[...], b_out[out_rows(core, place), :])

    ring = {}
    halves = (pl.ds(0, QROWS // 2), pl.ds(QROWS // 2, QROWS // 2))

    def send_sum(step, far):
        for way in range(2):
            half = way if far else 1 - way
            rows = halves[half]
            j = 0 if step == 0 else 2 * step - 1 + way
            if ("sib", j) not in seen:
                sib[j].wait_recv()
                seen.add(("sib", j))
            total = own[j % 3, rows] + sib_recv[j, rows].astype(F32)
            if (way, step - 1, half) in ring:
                ring[way, step - 1, half].wait_recv()
                total = total + ring_recv[way, step - 1, rows].astype(F32)
            ring_send[way, step, rows] = total.astype(BF16)
            copy = remote(
                ring_send.at[way, step, rows], ring_recv.at[way, step, rows],
                r_send.at[way, step, half], r_recv.at[way, step, half], toward[way],
            )
            copy.start()
            ring[way, step, half] = copy

    seen = set()
    compute(0)
    send_sum(0, True)
    compute(1)
    compute(2)
    for step in range(1, HOPS):
        send_sum(step, False)
        compute(2 * step + 1)
        send_sum(step, True)
        if step < HOPS - 1:
            compute(2 * step + 2)
    last = 2 * HOPS - 1
    sib[last].wait_recv()

    def chunk(place):
        cols = pl.ds(pl.multiple_of(place * CHUNK, 128), CHUNK)
        return gathered.at[pl.ds(0, QROWS), cols]

    spread = {}

    def part_of(place, half):
        cols = pl.ds(pl.multiple_of(place * CHUNK, 128), CHUNK)
        return gathered.at[halves[half], cols]

    def send_spread(way, step, half):
        if step == HOPS - 1 and half != way:
            return
        ref = part_of(at(-step if way == 0 else step), half)
        sems = g_send.at[way, step, half], g_recv.at[way, step, half]
        copy = remote(ref, ref, *sems, toward[way])
        copy.start()
        spread[way, step, half] = copy

    for half in (1, 0):
        ring[half ^ 1, HOPS - 1, half].wait_recv()
    for half in range(2):
        ring[half, HOPS - 1, half].wait_recv()
        rows = halves[half]
        part_of(pos, half)[...] = (
            own[last % 3, rows] + sib_recv[last, rows].astype(F32)
            + ring_recv[0, HOPS - 1, rows].astype(F32)
            + ring_recv[1, HOPS - 1, rows].astype(F32)
        ).astype(BF16)
    for turn in range(2):
        for way in range(2):
            send_spread(way, 0, (turn + way) % 2)
    for copy in keep:
        copy.wait()
    for copy in give:
        copy.wait()

    def multiply(place):
        block_of = chunk(place)
        t_in = pl.ds(pl.multiple_of(place * IN_CHUNK, 128), IN_CHUNK)
        t_out = pl.ds(pl.multiple_of(IN_HALF + place * OUT_CHUNK, 128), OUT_CHUNK)
        return (
            nt(traces[:, t_in], block_of[:, :IN_CHUNK]),
            nt(traces[:, t_out], block_of[:, IN_CHUNK:]),
        )

    pair[0], pair[1] = multiply(pos)
    for step in range(HOPS):
        for turn in range(2):
            for way in range(2):
                half = (turn + way) % 2
                if (way, step, half) in spread:
                    spread[way, step, half].wait_recv()
                    if step < HOPS - 1:
                        send_spread(way, step + 1, half)
        for way in range(2 if step < HOPS - 1 else 1):
            a, b = multiply(at(-1 - step if way == 0 else 1 + step))
            pair[0] += a
            pair[1] += b

    their_rows = pl.ds(pl.multiple_of(other * local_rows, local_rows), local_rows)
    swap = remote(pair.at[:, their_rows], pair_recv, p_send, p_recv, sibling)
    swap.start()
    swap.wait_recv()
    left = pair[0, t_rows, :] + pair_recv[0]
    right = pair[1, t_rows, :] + pair_recv[1]
    traces_here = local_rows // TTOK
    products = left * right
    sums = jnp.concatenate(
        [
            jnp.sum(products[i * TTOK : (i + 1) * TTOK], axis=0, keepdims=True)
            for i in range(traces_here)
        ],
        axis=0,
    )
    query_of = lax.broadcasted_iota(jnp.int32, (QUERIES, QROWS), 0) * QTOK
    token = lax.broadcasted_iota(jnp.int32, (QUERIES, QROWS), 1)
    select = jnp.where((token >= query_of) & (token < query_of + QTOK), 1.0, 0.0).astype(F32)
    scores = lax.dot_general(
        select, sums, (((1,), (1,)), ((), ())),
        precision=lax.Precision.HIGHEST, preferred_element_type=F32,
    )
    out[...] = scores * (1.0 / (math.sqrt(DA) * math.sqrt(FW) * TTOK * QTOK))

    swap.wait_send()
    for copy in sib:
        copy.wait_send()
    for copy in list(ring.values()) + list(spread.values()):
        copy.wait_send()


def per_device_ring(
    query_inputs, query_grads, basis_in, basis_out, eig_in, eig_out, trace_inputs, trace_grads
):
    spare = query_grads[:, TAIL:].reshape(GROUPS, SPARE, EXTRA).swapaxes(0, 1)
    query = jnp.concatenate(
        [
            jnp.concatenate([query_inputs, query_grads[:, :TAIL]], axis=1),
            spare.reshape(SPARE, WIDE),
        ],
        axis=0,
    )
    cin, cout = basis_in.shape[1], basis_out.shape[1]
    rows = trace_inputs.shape[0]
    dma = pltpu.SemaphoreType.DMA
    padded = CHIPS * CORES * PAD
    vmem = pl.BlockSpec(memory_space=pltpu.VMEM)
    hbm = pl.BlockSpec(memory_space=pl.ANY)
    return pl.pallas_call(
        kernel,
        out_shape=jax.ShapeDtypeStruct((QUERIES, rows // TTOK), F32),
        in_specs=[hbm, hbm, hbm, vmem, vmem, hbm, hbm],
        out_specs=vmem,
        scratch_shapes=[
            pltpu.VMEM((DA, cin), BF16),
            pltpu.VMEM((FW, cout), BF16),
            pltpu.VMEM((padded, WIDE), BF16),
            pltpu.VMEM((QROWS, EXTRA), BF16),
            pltpu.VMEM((PAD, EXTRA), F32),
            pltpu.VMEM((padded, cin), F32),
            pltpu.VMEM((padded, cout), F32),
            pltpu.VMEM((QROWS, cout), F32),
            pltpu.VMEM((QROWS, cin), BF16),
            pltpu.VMEM((QROWS, cout), BF16),
            pltpu.VMEM((CORES * rows, HALF), BF16),
            pltpu.VMEM((3, QROWS, CHUNK), F32),
            pltpu.VMEM((2 * HOPS, QROWS, CHUNK), BF16),
            pltpu.VMEM((2, HOPS, QROWS, CHUNK), BF16),
            pltpu.VMEM((2, HOPS, QROWS, CHUNK), BF16),
            pltpu.VMEM((2, CORES * rows, QROWS), F32),
            pltpu.VMEM((2, rows, QROWS), F32),
            dma((5,)),
            dma((2, 2, HOPS, 2)),
            dma((2, 2, HOPS, 2)),
            dma((2, 2 * HOPS, 2)),
            dma((2, 2 * HOPS, 2)),
            dma((2,)),
            dma((2,)),
            dma((2 * HOPS,)),
            dma((2 * HOPS,)),
            dma((2, HOPS, 2)),
            dma((2, HOPS, 2)),
            dma((2, HOPS, 2)),
            dma((2, HOPS, 2)),
            dma(()),
            dma(()),
        ],
        compiler_params=pltpu.CompilerParams(
            collective_id=0, has_side_effects=True, vmem_limit_bytes=63 * 1024 * 1024
        ),
        name="influence",
    )(
        query, basis_in, basis_out, eig_in, eig_out,
        trace_inputs, trace_grads,
    )


def per_device_plain(
    query_inputs, query_grads, basis_in, basis_out, eig_in, eig_out, trace_inputs, trace_grads
):
    def gather(x):
        return lax.all_gather(x, "basis", axis=0, tiled=True)

    def condition(query, basis, eig):
        rot = (jnp.dot(gather(query), basis, preferred_element_type=F32) / (eig + damping)).astype(
            BF16
        )
        share = lax.psum_scatter(
            jnp.dot(basis, rot.T, preferred_element_type=F32),
            "basis",
            scatter_dimension=0,
            tiled=True,
        )
        return gather(share.astype(BF16)).astype(F32)

    pre_in = condition(query_inputs, basis_in, eig_in)
    pre_grad = condition(query_grads, basis_out, eig_out)
    high = lax.Precision.HIGHEST
    pair_in = jnp.dot(trace_inputs.astype(F32), pre_in, precision=high) / math.sqrt(DA)
    pair_grad = jnp.dot(trace_grads.astype(F32), pre_grad, precision=high) / math.sqrt(FW)
    local_traces = trace_inputs.shape[0] // TTOK
    products = (pair_in * pair_grad).reshape(local_traces, TTOK, QUERIES, QTOK)
    return jnp.sum(products, axis=(1, 3)).T / (TTOK * QTOK)


def solution(mesh):
    fits = mesh.shape["basis"] == CHIPS * CORES
    return jax.shard_map(
        per_device_ring if fits else per_device_plain,
        mesh=mesh,
        in_specs=(
            P(("grp", "basis"), None),
            P(("grp", "basis"), None),
            P(None, "basis"),
            P(None, "basis"),
            P("basis"),
            P("basis"),
            P(("grp", "basis"), None),
            P(("grp", "basis"), None),
        ),
        out_specs=P(None, ("grp", "basis")),
        check_vma=False,
    )
```
